32 devices in a mesh: dp: 4 (over x, core), expert: 8 (over z, y).
Axes of the slice: x: 2, y: 2, z: 4, core: 2. Of those that a mesh axis runs over, the one named last changes fastest.
Arguments:
- tokens: bfloat16 [16384, 1024], P(('dp', 'expert')), may hold values from -6 to 6
- doc_lens: int32 [32, 8], P(('dp', 'expert')), may hold values from 0 to 512, as said below
- expert_picks: int32 [16384, 8], P(('dp', 'expert')), may hold values from 0 to 31, all different within a row; in each aligned block of 512 rows (0 to 511, 512 to 1023, ...) at most 192 rows name the same one
- gain_attn: float32 [1024], replicated, may hold values from 0.1 to 1.9
- w_query: bfloat16 [1024, 1024], replicated, may hold values from -0.1875 to 0.1875
- w_key: bfloat16 [1024, 512], replicated, may hold values from -0.1875 to 0.1875
- w_value: bfloat16 [1024, 512], replicated, may hold values from -0.1875 to 0.1875
- w_out: bfloat16 [1024, 1024], replicated, may hold values from -1.5 to 1.5
- gain_ffn: float32 [1024], replicated, may hold values from 0.1 to 1.9
- w_router: bfloat16 [1024, 32], replicated, may hold values from -0.09375 to 0.09375
- w_gate: bfloat16 [32, 1024, 512], P('expert'), may hold values from -0.1875 to 0.1875
- w_up: bfloat16 [32, 1024, 512], P('expert'), may hold values from -0.1875 to 0.1875
- w_down: bfloat16 [32, 512, 1024], P('expert'), may hold values from -0.75 to 0.75
- cotangent: bfloat16 [16384, 1024], P(('dp', 'expert')), may hold values from -6 to 6
Outputs:
- out_tokens: bfloat16 [16384, 1024], P(('dp', 'expert'))
- grad_tokens: bfloat16 [16384, 1024], P(('dp', 'expert'))
- grad_gain_attn: float32 [1024], replicated
- grad_query: float32 [1024, 1024], replicated
- grad_key: float32 [1024, 512], replicated
- grad_value: float32 [1024, 512], replicated
- grad_w_out: float32 [1024, 1024], replicated
- grad_gain_ffn: float32 [1024], replicated
- grad_router: float32 [1024, 32], replicated
- grad_gate: float32 [32, 1024, 512], P('expert', 'dp')
- grad_up: float32 [32, 1024, 512], P('expert', 'dp')
- grad_down: float32 [32, 512, 1024], P('expert', 'dp')
The draws below stay inside these ranges and needn't reach their ends.
Inputs may be any that keep to these rules, and one draw needn't show every extreme that they name: `doc_lens`: each device's 8 lengths sum to 512; on some device one document fills all 512 tokens. `expert_picks`: A token's 8 experts differ; the rows of one device name one expert at most 192 times, a bound that some block reaches.
All inputs are finite; a program needn't handle non-finite values.
Results may differ from the reference program's by a relative error of at most 0.013.
The reference program's roundings to bfloat16 on the way count: a program that leaves them out, or rounds other values in their place, can miss the bound.
Values may be sent and summed in bfloat16 or wider, within the bound.
A program may use at most 256 MiB of HBM per device.

```python
import math
import jax
import jax.numpy as jnp
import numpy as np
from jax import lax

D = 1024
H = 16
KVH = 8
HD = 64
F = 512
EXPERTS = 32
TOP = 8
TOK_DEV = 512
DOCS = 8
CAP = 192
TOKENS = 16384
DEVICES = 32


def draw_doc_lens(key, part):
    key = jax.random.fold_in(key, 11)
    key_cuts, key_full = jax.random.split(key)
    cut_points = jnp.sort(jax.random.randint(key_cuts, (DEVICES, DOCS - 1), 0, TOK_DEV + 1), axis=1).astype(jnp.int32)
    boundary = jnp.concatenate([jnp.zeros((DEVICES, 1), jnp.int32), cut_points, jnp.full((DEVICES, 1), TOK_DEV, jnp.int32)], axis=1)
    lengths = boundary[:, 1:] - boundary[:, :-1]
    full_device = jax.random.randint(key_full, (), 0, DEVICES)
    single = (jnp.arange(DOCS) == 0).astype(jnp.int32) * TOK_DEV
    return jnp.where((jnp.arange(DEVICES) == full_device)[:, None], single[None, :], lengths).astype(jnp.int32)


def shard_levels(stream_key, shape, shards, smallest, high):
    loudness, own = 1.0, jax.random.fold_in(stream_key, 6)
    for dim, parts in shards:
        heights = jnp.exp(jax.random.uniform(jax.random.fold_in(own, dim), (parts,), jnp.float32, smallest / len(shards), high / len(shards)))
        loudness = loudness * jnp.repeat(heights, shape[dim] // parts).reshape([-1 if axis == dim else 1 for axis in range(len(shape))])
    return loudness


def routed_block(rng, own, number, rows, number_of, top, most, skew):
    sequence = jax.random.permutation(rng, number_of)
    crowded, common = portions_of(number_of, rows * top, most, skew, True), portions_of(number_of, rows * top, most, skew, False)
    places = jnp.arange(number_of)

    def named(tallies, rotation):
        used = int((tallies > 0).sum())
        fixed = max(1, used // 4)
        moved = fixed + (places - fixed + rotation * (used - fixed)) % max(1, number_of - fixed)
        return jnp.zeros((number_of,), jnp.int32).at[sequence[jnp.where(places < fixed, places, moved)]].set(jnp.asarray(tallies, jnp.int32))

    tallies = jnp.where(number % 4 == 0, named(crowded, number // 4), named(common, number - number // 4 - 1))
    mixed = jax.random.permutation(jax.random.fold_in(own, 3), number_of)
    source_of, sink = mixed[0:number_of // 2 * 2:2], mixed[1:number_of // 2 * 2:2]
    slack = jnp.minimum(tallies[source_of] - 1, most - tallies[sink]) // 2
    slack = jnp.where((source_of == sequence[0]) | (sink == sequence[0]) | (tallies[sink] == 0), 0, jnp.maximum(slack, 0))
    moved = jax.random.randint(jax.random.fold_in(own, 4), (number_of // 2,), 0, 1 << 20) % (slack + 1)
    tallies = tallies.at[source_of].add(-moved).at[sink].add(moved)
    items = jnp.searchsorted(jnp.cumsum(tallies), jnp.arange(rows * top), side="right").astype(jnp.int32)
    grid = items.reshape(top, rows).T
    grid = grid[jax.random.permutation(jax.random.fold_in(own, 1), rows)]
    rotation = jax.random.randint(jax.random.fold_in(own, 2), (rows, 1), 0, top)
    return jnp.take_along_axis(grid, (jnp.arange(top)[None, :] + rotation) % top, axis=1)


def portions_of(amount, total, bound, slope, full):
    weights = [(1 << 20) // math.isqrt(grade ** slope) + 1 for grade in range(1, amount + 1)]
    largest = bound if full else min(bound, max(-(-total // amount), total * weights[0] // sum(weights)))
    least = 1 if total - largest >= amount - 1 else 0
    given, surplus = [largest] + [least] * (amount - 1), total - largest - least * (amount - 1)
    while surplus > 0:
        free = [i for i in range(1, amount) if given[i] < largest] or [i for i in range(1, amount) if given[i] < bound]
        pool, budget = sum([weights[i] for i in free]), surplus
        for i in free:
            extra = min(bound - given[i], max(1, budget * weights[i] // pool), surplus)
            given[i] = given[i] + extra
            surplus = surplus - extra
    return np.array(given)


def gaussian(own_key, dims, spread, most, cuts=(), held_as=jnp.bfloat16):
    factor_of = shard_levels(own_key, dims, cuts, -0.22, 0.18) if cuts else 1.0
    values = jax.random.normal(own_key, dims, jnp.float32) * spread * factor_of
    return jnp.minimum(jnp.maximum(values, -most), most).astype(held_as)


def setup_inputs(seed: int = 0) -> dict:
    keys = jax.random.split(jax.random.key(seed), 15)
    tokens = gaussian(keys[0], (TOKENS, D), 1.0, 6.0, ((0, 32),))
    doc_lens = draw_doc_lens(jax.random.fold_in(keys[14], 71), 0)
    expert_picks_keys = jax.random.split(jax.random.fold_in(keys[2], 1), TOKENS // TOK_DEV)
    expert_picks_turns = jax.random.permutation(jax.random.fold_in(keys[2], 3), TOKENS // TOK_DEV)
    expert_picks = jax.vmap(lambda own, number: routed_block(jax.random.fold_in(keys[2], 2), own, number, TOK_DEV, EXPERTS, TOP, CAP, 1))(expert_picks_keys, expert_picks_turns).reshape((TOKENS, TOP))
    gain_attn = jnp.clip(1.0 + 0.18 * jax.random.normal(keys[3], (D,), jnp.float32), 0.1, 1.9)
    w_query = gaussian(keys[4], (D, H * HD), D ** -0.5, 0.1875)
    w_key = gaussian(keys[5], (D, KVH * HD), D ** -0.5, 0.1875)
    w_value = gaussian(keys[6], (D, KVH * HD), D ** -0.5, 0.1875)
    w_out = gaussian(keys[7], (H * HD, D), (D // 64) ** -0.5, 1.5)
    gain_ffn = jnp.clip(1.0 + 0.18 * jax.random.normal(keys[8], (D,), jnp.float32), 0.1, 1.9)
    w_router = gaussian(keys[9], (D, EXPERTS), (4 * D) ** -0.5, 0.09375)
    w_gate = gaussian(keys[10], (EXPERTS, D, F), D ** -0.5, 0.1875, ((0, 8),))
    w_up = gaussian(keys[11], (EXPERTS, D, F), D ** -0.5, 0.1875, ((0, 8),))
    w_down = gaussian(keys[12], (EXPERTS, F, D), (F // 8) ** -0.5, 0.75, ((0, 8),))
    cotangent = gaussian(keys[13], (TOKENS, D), 1.0, 6.0, ((0, 32),))
    return dict(tokens=tokens, doc_lens=doc_lens, expert_picks=expert_picks, gain_attn=gain_attn, w_query=w_query, w_key=w_key, w_value=w_value, w_out=w_out, gain_ffn=gain_ffn, w_router=w_router, w_gate=w_gate, w_up=w_up, w_down=w_down, cotangent=cotangent)


@jax.custom_vjp
def low(v):
    return lax.optimization_barrier(v.astype(jnp.bfloat16)).astype(jnp.float32)

@jax.custom_vjp
def low_back(v):
    return v

def low_keep(v):
    return (low(v), None)

def low_pass(kept, grad):
    return (grad,)

def back_keep(v):
    return (v, None)

def back_low(kept, grad):
    return (low(grad),)
low.defvjp(low_keep, low_pass)
low_back.defvjp(back_keep, back_low)
epsilon = 1e-06
theta_base = 10000.0

def matmul_high(left, right):
    return jnp.dot(left, right, precision=lax.Precision.HIGHEST, preferred_element_type=jnp.float32)

def doc_layout(lengths):
    ends_at = jnp.cumsum(lengths, dtype=jnp.int32)
    places = jnp.arange(TOK_DEV, dtype=jnp.int32)
    passed = ends_at[None, :] <= places[:, None]
    segment = lax.optimization_barrier(jnp.sum(passed.astype(jnp.int32), axis=1, dtype=jnp.int32))
    start_at = lax.optimization_barrier(jnp.sum(jnp.where(passed, lengths[None, :], 0), axis=1, dtype=jnp.int32))
    return (segment, places - start_at)

def rope_tables(position):
    freqs = theta_base ** (-2.0 * jnp.arange(HD // 2, dtype=jnp.float32) / HD)
    angles = position.astype(jnp.float32)[:, None] * freqs[None, :]
    return (jnp.cos(angles), jnp.sin(angles))

def rotate(field, cosine, sine_part):
    half_width = field.shape[-1] // 2
    first_half = field[..., :half_width]
    second_half = field[..., half_width:]
    cos_b = cosine[:, None, :]
    sin_b = sine_part[:, None, :]
    return jnp.concatenate([first_half * cos_b - second_half * sin_b, second_half * cos_b + first_half * sin_b], axis=-1)

def attend_device(inputs, lengths, gain_attn, w_query, w_key, w_value, w_out, gain_ffn, w_router):
    segment, position = doc_layout(lengths)
    cosine, sine_part = rope_tables(position)
    scale_attn = lax.rsqrt(lax.optimization_barrier(jnp.mean(inputs * inputs, axis=1, keepdims=True)) + epsilon)
    normed_attn = low(inputs * scale_attn * gain_attn)
    queries = low(rotate(low_back(matmul_high(normed_attn, w_query)).reshape(TOK_DEV, H, HD), cosine, sine_part))
    key_rows = low(rotate(low_back(matmul_high(normed_attn, w_key)).reshape(TOK_DEV, KVH, HD), cosine, sine_part))
    value_rows = low(low_back(matmul_high(normed_attn, w_value))).reshape(TOK_DEV, KVH, HD)
    queries = queries.reshape(TOK_DEV, KVH, H // KVH, HD)
    scores = low_back(jnp.einsum('qgrd,kgd->grqk', queries, key_rows, precision=lax.Precision.HIGHEST) * 0.125)
    places = jnp.arange(TOK_DEV, dtype=jnp.int32)
    allowed = (segment[:, None] == segment[None, :]) & (places[None, :] <= places[:, None])
    scores = jnp.where(allowed, scores, -1e+30)
    maxima = lax.optimization_barrier(jnp.max(scores, axis=-1, keepdims=True))
    exponent = jnp.exp(scores - maxima)
    attn_probs = exponent / lax.optimization_barrier(jnp.sum(exponent, axis=-1, keepdims=True))
    attended = jnp.einsum('grqk,kgd->qgrd', low(attn_probs), value_rows, precision=lax.Precision.HIGHEST)
    attended = low(low_back(attended.reshape(TOK_DEV, H * HD)))
    residual = inputs + low_back(matmul_high(attended, w_out))
    scale_ffn = lax.rsqrt(lax.optimization_barrier(jnp.mean(residual * residual, axis=1, keepdims=True)) + epsilon)
    normed_ffn = low(residual * scale_ffn * gain_ffn)
    logits = low_back(matmul_high(normed_ffn, w_router))
    return (residual, normed_ffn, logits)

def gate_weights(logits, picks):
    is_chosen = picks[:, :, None] == jnp.arange(EXPERTS, dtype=jnp.int32)[None, None, :]
    chosen = lax.optimization_barrier(jnp.sum(jnp.where(is_chosen, logits[:, None, :], 0.0), axis=2))
    maxima = lax.optimization_barrier(jnp.max(chosen, axis=1, keepdims=True))
    exponent = jnp.exp(chosen - maxima)
    return exponent / lax.optimization_barrier(jnp.sum(exponent, axis=1, keepdims=True))

def slot_table(picks):
    flat_picks = picks.reshape(-1)
    hits = (flat_picks[:, None] == jnp.arange(EXPERTS, dtype=jnp.int32)[None, :]).astype(jnp.int32)
    earlier = jnp.cumsum(hits, axis=0, dtype=jnp.int32) - hits
    ranks = lax.optimization_barrier(jnp.sum(earlier * hits, axis=1, dtype=jnp.int32))
    slot_of = flat_picks * CAP + ranks
    token_of = jnp.arange(flat_picks.shape[0], dtype=jnp.int32) // TOP
    slot_owner = jnp.full((EXPERTS * CAP,), TOK_DEV, jnp.int32).at[slot_of].set(token_of)
    return (slot_of.reshape(TOK_DEV, TOP), slot_owner)

def take_rows(source, lookup):
    return source[lookup]

def expert_apply(packed):
    arrived, gate_mat, up_mat, down_mat = packed
    arrived = arrived.reshape(DEVICES * CAP, D)
    gate_pre = low_back(matmul_high(arrived, gate_mat))
    up_pre = low_back(matmul_high(arrived, up_mat))
    hidden = low(jax.nn.silu(gate_pre) * up_pre)
    return low(low_back(matmul_high(hidden, down_mat))).reshape(DEVICES, CAP, D)

def forward(inputs, gain_attn, w_query, w_key, w_value, w_out, gain_ffn, w_router, w_gate, w_up, w_down, doc_lens, expert_picks):
    per_device = jax.checkpoint(attend_device)

    def one_device(packed):
        return per_device(packed[0], packed[1], gain_attn, w_query, w_key, w_value, w_out, gain_ffn, w_router)
    residual, normed_ffn, logits = lax.map(one_device, (inputs.reshape(DEVICES, TOK_DEV, D), doc_lens))
    picks = expert_picks.reshape(DEVICES, TOK_DEV, TOP)
    gate_vals = jax.vmap(gate_weights)(logits, picks)
    slot_of, slot_owner = jax.vmap(slot_table)(picks)
    padded = jnp.concatenate([normed_ffn, jnp.zeros((DEVICES, 1, D), jnp.float32)], axis=1)
    dispatched = low_back(jax.vmap(take_rows)(padded, slot_owner))
    dispatched = dispatched.reshape(DEVICES, EXPERTS, CAP, D).transpose(1, 0, 2, 3)
    expert_out = lax.map(jax.checkpoint(expert_apply), (dispatched, w_gate, w_up, w_down))
    expert_out = expert_out.transpose(1, 0, 2, 3).reshape(DEVICES, EXPERTS * CAP, D)
    picked = jax.vmap(take_rows)(expert_out, slot_of)
    expert_sum = jnp.einsum('nst,nstd->nsd', gate_vals, picked, precision=lax.Precision.HIGHEST)
    return (residual + expert_sum).reshape(DEVICES * TOK_DEV, D)

def reference(tokens, doc_lens, expert_picks, gain_attn, w_query, w_key, w_value, w_out, gain_ffn, w_router, w_gate, w_up, w_down, cotangent):
    floats = tuple((item.astype(jnp.float32) for item in (tokens, gain_attn, w_query, w_key, w_value, w_out, gain_ffn, w_router, w_gate, w_up, w_down)))

    def run_layer(*weights):
        return forward(*weights, doc_lens, expert_picks)
    result, pull_back = jax.vjp(run_layer, *floats)
    grads = pull_back(cotangent.astype(jnp.float32))
    return (result.astype(jnp.bfloat16), grads[0].astype(jnp.bfloat16), grads[1], grads[2], grads[3], grads[4], grads[5], grads[6], grads[7], grads[8], grads[9], grads[10])
```

```python
import jax
import jax.numpy as jnp
from jax import lax
from jax.sharding import PartitionSpec as P

HD = 64
EXPERTS = 32
TOP = 8
CAP = 192


epsilon = 1e-06
theta_base = 10000.0


def doc_layout(lengths, tok_rows):
    ends_at = jnp.cumsum(lengths, dtype=jnp.int32)
    places = jnp.arange(tok_rows, dtype=jnp.int32)
    passed = ends_at[None, :] <= places[:, None]
    segment = jnp.sum(passed.astype(jnp.int32), axis=1, dtype=jnp.int32)
    start_at = jnp.sum(jnp.where(passed, lengths[None, :], 0), axis=1, dtype=jnp.int32)
    return (segment, places - start_at)


def rope_tables(position, head_size):
    freqs = theta_base ** (-2.0 * jnp.arange(head_size // 2, dtype=jnp.float32) / head_size)
    angles = position.astype(jnp.float32)[:, None] * freqs[None, :]
    return (jnp.cos(angles), jnp.sin(angles))


def rotate(field, cosine, sine_part):
    half_width = field.shape[-1] // 2
    first_half = field[..., :half_width]
    second_half = field[..., half_width:]
    cos_b = cosine[:, None, :]
    sin_b = sine_part[:, None, :]
    return jnp.concatenate(
        [first_half * cos_b - second_half * sin_b, second_half * cos_b + first_half * sin_b],
        axis=-1,
    )


def rms_scale(field):
    return lax.rsqrt(jnp.mean(field * field, axis=1, keepdims=True) + epsilon)


def rms_back(field, scale, gain, grad_normed):
    normed = field * scale
    grad_scaled = grad_normed * gain
    grad_field = scale * (
        grad_scaled - normed * jnp.mean(grad_scaled * normed, axis=1, keepdims=True)
    )
    return (grad_field, jnp.sum(grad_normed * normed, axis=0))


def masked_scores(queries, key_rows, allowed):
    scores = (
        jnp.einsum("qgrd,kgd->grqk", queries, key_rows, preferred_element_type=jnp.float32) * 0.125
    )
    return jnp.where(allowed, scores, -1e30)


def expert_forward(arrived, w_gate, w_up):
    gate_pre = jnp.einsum("secd,edf->secf", arrived, w_gate, preferred_element_type=jnp.float32)
    up_pre = jnp.einsum("secd,edf->secf", arrived, w_up, preferred_element_type=jnp.float32)
    hidden = (jax.nn.silu(gate_pre) * up_pre).astype(jnp.bfloat16)
    return (gate_pre, up_pre, hidden)


def shards(
    tokens,
    doc_lens,
    expert_picks,
    gain_attn,
    w_query,
    w_key,
    w_value,
    w_out,
    gain_ffn,
    w_router,
    w_gate,
    w_up,
    w_down,
    cotangent,
):
    tok_rows = tokens.shape[0]
    width = tokens.shape[1]
    local_experts = w_gate.shape[0]
    owner_count = lax.axis_size("expert")
    head_count = w_query.shape[1] // HD
    group_count = w_key.shape[1] // HD
    group_size = head_count // group_count
    owner = lax.axis_index("expert")
    cot_all = lax.all_gather(cotangent, "expert")
    picks_all = lax.all_gather(expert_picks.T, "expert")
    segment, position = doc_layout(doc_lens[0], tok_rows)
    cosine, sine_part = rope_tables(position, HD)
    places = jnp.arange(tok_rows, dtype=jnp.int32)
    allowed = (segment[:, None] == segment[None, :]) & (places[None, :] <= places[:, None])
    inputs = tokens.astype(jnp.float32)
    scale_attn = rms_scale(inputs)
    normed_attn = (inputs * scale_attn * gain_attn).astype(jnp.bfloat16)
    queries = rotate(
        jnp.dot(normed_attn, w_query, preferred_element_type=jnp.float32).reshape(
            tok_rows, head_count, HD
        ),
        cosine,
        sine_part,
    )
    queries = queries.astype(jnp.bfloat16).reshape(tok_rows, group_count, group_size, HD)
    key_rows = rotate(
        jnp.dot(normed_attn, w_key, preferred_element_type=jnp.float32).reshape(
            tok_rows, group_count, HD
        ),
        cosine,
        sine_part,
    ).astype(jnp.bfloat16)
    value_rows = (
        jnp.dot(normed_attn, w_value, preferred_element_type=jnp.float32)
        .astype(jnp.bfloat16)
        .reshape(tok_rows, group_count, HD)
    )
    scores = masked_scores(queries, key_rows, allowed)
    maxima = jnp.max(scores, axis=-1, keepdims=True)
    exponent = jnp.exp(scores - maxima)
    totals = jnp.sum(exponent, axis=-1, keepdims=True)
    log_totals = maxima + jnp.log(totals)
    attn_probs = (exponent / totals).astype(jnp.bfloat16)
    attended = jnp.einsum(
        "grqk,kgd->qgrd", attn_probs, value_rows, preferred_element_type=jnp.float32
    )
    attended = attended.reshape(tok_rows, head_count * HD).astype(jnp.bfloat16)
    residual = inputs + jnp.dot(attended, w_out, preferred_element_type=jnp.float32)
    scale_ffn = rms_scale(residual)
    normed_ffn = (residual * scale_ffn * gain_ffn).astype(jnp.bfloat16)
    normed_all = lax.all_gather(normed_ffn, "expert")
    earlier = (places[:, None] < places[None, :]).astype(jnp.bfloat16)
    expert_ids = jnp.arange(EXPERTS, dtype=jnp.int32)
    chosen = jnp.any(picks_all[:, :, None, :] == expert_ids[None, None, :, None], axis=1)
    own_ids = owner * local_experts
    hits = lax.dynamic_slice_in_dim(chosen, own_ids, local_experts, axis=1)
    ranks = jnp.einsum(
        "set,tu->seu", hits.astype(jnp.bfloat16), earlier, preferred_element_type=jnp.float32
    ).astype(jnp.int32)
    ranks = jnp.where(hits, ranks, -1)
    takes = ranks[:, :, None, :] == jnp.arange(CAP, dtype=jnp.int32)[None, None, :, None]
    one_hot = takes.astype(jnp.bfloat16)
    grad_taken = jnp.einsum(
        "sect,std->secd", one_hot, cot_all, preferred_element_type=jnp.float32
    ).astype(jnp.bfloat16)
    logits = jnp.einsum("std,de->set", normed_all, w_router, preferred_element_type=jnp.float32)
    logits = jnp.where(chosen, logits, -1e30)
    gate_exp = jnp.exp(logits - jnp.max(logits, axis=1, keepdims=True))
    gate_exp = jnp.where(chosen, gate_exp, 0.0)
    gates = gate_exp / jnp.sum(gate_exp, axis=1, keepdims=True)
    own_gates = lax.dynamic_slice_in_dim(gates, own_ids, local_experts, axis=1)
    gated = jnp.where(takes, own_gates[:, :, None, :], 0.0)
    slot_gate = jnp.sum(gated, axis=3)
    arrived = jnp.einsum(
        "sect,std->secd", one_hot, normed_all, preferred_element_type=jnp.float32
    ).astype(jnp.bfloat16)
    gate_pre, up_pre, hidden = expert_forward(arrived, w_gate, w_up)
    result = jnp.einsum(
        "secf,efd->secd", hidden, w_down, preferred_element_type=jnp.float32
    ).astype(jnp.bfloat16)
    expert_part = jnp.einsum(
        "sect,secd->std", gated.astype(jnp.bfloat16), result, preferred_element_type=jnp.float32
    ).astype(jnp.bfloat16)
    expert_sum = lax.psum_scatter(
        expert_part.reshape(owner_count * tok_rows, width),
        "expert",
        scatter_dimension=0,
        tiled=True,
    )
    out_tokens = (residual + expert_sum.astype(jnp.float32)).astype(jnp.bfloat16)
    grad_flow = cotangent.astype(jnp.float32)
    slot_dots = jnp.sum(grad_taken.astype(jnp.float32) * result.astype(jnp.float32), axis=3)
    grad_gates = jnp.sum(jnp.where(takes, slot_dots[:, :, :, None], 0.0), axis=2)
    grad_gates = lax.all_to_all(grad_gates, "expert", split_axis=0, concat_axis=0, tiled=True)
    grad_gates = grad_gates.reshape(EXPERTS, tok_rows)
    back_grad = (grad_taken.astype(jnp.float32) * slot_gate[:, :, :, None]).astype(jnp.bfloat16)
    grad_hidden = jnp.einsum(
        "secd,efd->secf", back_grad, w_down, preferred_element_type=jnp.float32
    )
    sigmoid_gate = jax.nn.sigmoid(gate_pre)
    grad_gate_pre = (
        grad_hidden * up_pre * sigmoid_gate * (1.0 + gate_pre * (1.0 - sigmoid_gate))
    ).astype(jnp.bfloat16)
    grad_up_pre = (grad_hidden * gate_pre * sigmoid_gate).astype(jnp.bfloat16)
    grad_slots = jnp.einsum(
        "secf,edf->secd", grad_gate_pre, w_gate, preferred_element_type=jnp.float32
    )
    grad_slots = (
        grad_slots
        + jnp.einsum("secf,edf->secd", grad_up_pre, w_up, preferred_element_type=jnp.float32)
    ).astype(jnp.bfloat16)
    grad_part = jnp.einsum(
        "sect,secd->std", one_hot, grad_slots, preferred_element_type=jnp.float32
    ).astype(jnp.bfloat16)
    grad_rows = lax.psum_scatter(
        grad_part.reshape(owner_count * tok_rows, width),
        "expert",
        scatter_dimension=0,
        tiled=True,
    )
    grad_down = jnp.einsum("secf,secd->efd", hidden, back_grad, preferred_element_type=jnp.float32)
    grad_gate = jnp.einsum(
        "secd,secf->edf", arrived, grad_gate_pre, preferred_element_type=jnp.float32
    )
    grad_up = jnp.einsum("secd,secf->edf", arrived, grad_up_pre, preferred_element_type=jnp.float32)
    grad_gate, grad_up, grad_down = (
        lax.psum_scatter(
            grad_gate.astype(jnp.bfloat16), "dp", scatter_dimension=1, tiled=True
        ).astype(jnp.float32),
        lax.psum_scatter(
            grad_up.astype(jnp.bfloat16), "dp", scatter_dimension=1, tiled=True
        ).astype(jnp.float32),
        lax.psum_scatter(
            grad_down.astype(jnp.bfloat16), "dp", scatter_dimension=1, tiled=True
        ).astype(jnp.float32),
    )
    gate_vals = lax.dynamic_index_in_dim(gates, owner, axis=0, keepdims=False)
    grad_logits = (
        gate_vals * (grad_gates - jnp.sum(gate_vals * grad_gates, axis=0, keepdims=True))
    ).astype(jnp.bfloat16)
    grad_router = jnp.einsum(
        "et,td->ed", grad_logits, normed_ffn, preferred_element_type=jnp.float32
    )
    grad_normed_ffn = jnp.einsum(
        "et,de->td", grad_logits, w_router, preferred_element_type=jnp.float32
    )
    grad_normed_ffn = grad_normed_ffn + grad_rows.astype(jnp.float32)
    grad_norm_part, grad_gain_ffn = rms_back(residual, scale_ffn, gain_ffn, grad_normed_ffn)
    grad_residual = grad_flow + grad_norm_part
    grad_branch = grad_residual.astype(jnp.bfloat16)
    grad_w_out = jnp.einsum("se,sd->ed", attended, grad_branch, preferred_element_type=jnp.float32)
    both = ("dp", "expert")
    grad_w_out = lax.psum(grad_w_out.astype(jnp.bfloat16), both)
    small = jnp.concatenate(
        [grad_router, jnp.broadcast_to(grad_gain_ffn[None, :], (8, width))], axis=0
    )
    grad_attended = jnp.einsum("sd,ed->se", grad_branch, w_out, preferred_element_type=jnp.float32)
    grad_attended = grad_attended.astype(jnp.bfloat16).reshape(
        tok_rows, group_count, group_size, HD
    )
    again_probs = jnp.exp(masked_scores(queries, key_rows, allowed) - log_totals)
    grad_probs = jnp.einsum(
        "qgrd,kgd->grqk", grad_attended, value_rows, preferred_element_type=jnp.float32
    )
    grad_scores = (
        again_probs * (grad_probs - jnp.sum(again_probs * grad_probs, axis=-1, keepdims=True))
    ).astype(jnp.bfloat16)
    grad_q = (
        jnp.einsum("grqk,kgd->qgrd", grad_scores, key_rows, preferred_element_type=jnp.float32)
        * 0.125
    )
    grad_k = (
        jnp.einsum("grqk,qgrd->kgd", grad_scores, queries, preferred_element_type=jnp.float32)
        * 0.125
    )
    grad_v = jnp.einsum(
        "grqk,qgrd->kgd",
        again_probs.astype(jnp.bfloat16),
        grad_attended,
        preferred_element_type=jnp.float32,
    )
    grad_q = (
        rotate(grad_q.reshape(tok_rows, head_count, HD), cosine, -sine_part)
        .reshape(tok_rows, head_count * HD)
        .astype(jnp.bfloat16)
    )
    grad_k = (
        rotate(grad_k, cosine, -sine_part).reshape(tok_rows, group_count * HD).astype(jnp.bfloat16)
    )
    grad_v = grad_v.reshape(tok_rows, group_count * HD).astype(jnp.bfloat16)
    grad_query = jnp.einsum("sd,se->de", normed_attn, grad_q, preferred_element_type=jnp.float32)
    grad_key = jnp.einsum("sd,se->de", normed_attn, grad_k, preferred_element_type=jnp.float32)
    grad_value = jnp.einsum("sd,se->de", normed_attn, grad_v, preferred_element_type=jnp.float32)
    grad_normed_attn = jnp.einsum("se,de->sd", grad_q, w_query, preferred_element_type=jnp.float32)
    grad_normed_attn = grad_normed_attn + jnp.einsum(
        "se,de->sd", grad_k, w_key, preferred_element_type=jnp.float32
    )
    grad_normed_attn = grad_normed_attn + jnp.einsum(
        "se,de->sd", grad_v, w_value, preferred_element_type=jnp.float32
    )
    grad_input_part, grad_gain_attn = rms_back(inputs, scale_attn, gain_attn, grad_normed_attn)
    grad_tokens = (grad_residual + grad_input_part).astype(jnp.bfloat16)
    small = lax.psum(small, both)
    grad_router, grad_gain_ffn = small[:EXPERTS].T, small[EXPERTS]
    late = jnp.concatenate(
        [
            grad_query,
            jnp.concatenate([grad_key, grad_value], axis=1),
            jnp.broadcast_to(grad_gain_attn[None, :], (16, width)),
        ],
        axis=0,
    ).astype(jnp.bfloat16)
    late, grad_w_out = lax.optimization_barrier((late, grad_w_out))
    grad_w_out = grad_w_out.astype(jnp.float32)
    late = lax.psum(late, both).astype(jnp.float32)
    grad_query = late[:width]
    grad_key = late[width : 2 * width, : grad_key.shape[1]]
    grad_value = late[width : 2 * width, grad_key.shape[1] :]
    grad_gain_attn = late[2 * width]
    return (
        out_tokens,
        grad_tokens,
        grad_gain_attn,
        grad_query,
        grad_key,
        grad_value,
        grad_w_out,
        grad_gain_ffn,
        grad_router,
        grad_gate,
        grad_up,
        grad_down,
    )


def solution(mesh):
    placed = (
        P(("dp", "expert"), None),
        P(("dp", "expert"), None),
        P(("dp", "expert"), None),
        P(),
        P(),
        P(),
        P(),
        P(),
        P(),
        P(),
        P("expert", None, None),
        P("expert", None, None),
        P("expert", None, None),
        P(("dp", "expert"), None),
    )
    return jax.shard_map(
        shards,
        mesh=mesh,
        in_specs=placed,
        out_specs=(
            P(("dp", "expert"), None),
            P(("dp", "expert"), None),
            P(),
            P(),
            P(),
            P(),
            P(),
            P(),
            P(),
            P("expert", "dp", None),
            P("expert", "dp", None),
            P("expert", "dp", None),
        ),
        check_vma=False,
    )
```

```python
import jax
import jax.numpy as jnp
from jax import lax
from jax.sharding import PartitionSpec as P

HD = 64
EXPERTS = 32
TOP = 8
CAP = 192


epsilon = 1e-06
theta_base = 10000.0


def doc_layout(lengths, tok_rows):
    ends_at = jnp.cumsum(lengths, dtype=jnp.int32)
    places = jnp.arange(tok_rows, dtype=jnp.int32)
    passed = ends_at[None, :] <= places[:, None]
    segment = jnp.sum(passed.astype(jnp.int32), axis=1, dtype=jnp.int32)
    start_at = jnp.sum(jnp.where(passed, lengths[None, :], 0), axis=1, dtype=jnp.int32)
    return (segment, places - start_at)


def rope_tables(position, head_size):
    freqs = theta_base ** (-2.0 * jnp.arange(head_size // 2, dtype=jnp.float32) / head_size)
    angles = position.astype(jnp.float32)[:, None] * freqs[None, :]
    return (jnp.cos(angles), jnp.sin(angles))


def rotate(field, cosine, sine_part):
    half_width = field.shape[-1] // 2
    first_half = field[..., :half_width]
    second_half = field[..., half_width:]
    cos_b = cosine[:, None, :]
    sin_b = sine_part[:, None, :]
    return jnp.concatenate(
        [first_half * cos_b - second_half * sin_b, second_half * cos_b + first_half * sin_b],
        axis=-1,
    )


def rms_scale(field):
    return lax.rsqrt(jnp.mean(field * field, axis=1, keepdims=True) + epsilon)


def rms_back(field, scale, gain, grad_normed):
    normed = field * scale
    grad_scaled = grad_normed * gain
    grad_field = scale * (
        grad_scaled - normed * jnp.mean(grad_scaled * normed, axis=1, keepdims=True)
    )
    return (grad_field, jnp.sum(grad_normed * normed, axis=0))


def masked_scores(queries, key_rows, allowed):
    scores = (
        jnp.einsum("qgrd,kgd->grqk", queries, key_rows, preferred_element_type=jnp.float32) * 0.125
    )
    return jnp.where(allowed, scores, -1e30)


def expert_forward(arrived, w_gate, w_up):
    gate_pre = jnp.einsum("secd,edf->secf", arrived, w_gate, preferred_element_type=jnp.float32)
    up_pre = jnp.einsum("secd,edf->secf", arrived, w_up, preferred_element_type=jnp.float32)
    hidden = (jax.nn.silu(gate_pre) * up_pre).astype(jnp.bfloat16)
    return (gate_pre, up_pre, hidden)


def shards(
    tokens,
    doc_lens,
    expert_picks,
    gain_attn,
    w_query,
    w_key,
    w_value,
    w_out,
    gain_ffn,
    w_router,
    w_gate,
    w_up,
    w_down,
    cotangent,
):
    tok_rows = tokens.shape[0]
    width = tokens.shape[1]
    local_experts = w_gate.shape[0]
    owner_count = lax.axis_size("expert")
    head_count = w_query.shape[1] // HD
    group_count = w_key.shape[1] // HD
    group_size = head_count // group_count
    owner = lax.axis_index("expert")
    cot_all = lax.all_gather(cotangent, "expert")
    picks_all = lax.all_gather(expert_picks.T, "expert")
    segment, position = doc_layout(doc_lens[0], tok_rows)
    cosine, sine_part = rope_tables(position, HD)
    places = jnp.arange(tok_rows, dtype=jnp.int32)
    allowed = (segment[:, None] == segment[None, :]) & (places[None, :] <= places[:, None])
    inputs = tokens.astype(jnp.float32)
    scale_attn = rms_scale(inputs)
    normed_attn = (inputs * scale_attn * gain_attn).astype(jnp.bfloat16)
    queries = rotate(
        jnp.dot(normed_attn, w_query, preferred_element_type=jnp.float32).reshape(
            tok_rows, head_count, HD
        ),
        cosine,
        sine_part,
    )
    queries = queries.astype(jnp.bfloat16).reshape(tok_rows, group_count, group_size, HD)
    key_rows = rotate(
        jnp.dot(normed_attn, w_key, preferred_element_type=jnp.float32).reshape(
            tok_rows, group_count, HD
        ),
        cosine,
        sine_part,
    ).astype(jnp.bfloat16)
    value_rows = (
        jnp.dot(normed_attn, w_value, preferred_element_type=jnp.float32)
        .astype(jnp.bfloat16)
        .reshape(tok_rows, group_count, HD)
    )
    scores = masked_scores(queries, key_rows, allowed)
    maxima = jnp.max(scores, axis=-1, keepdims=True)
    exponent = jnp.exp(scores - maxima)
    totals = jnp.sum(exponent, axis=-1, keepdims=True)
    log_totals = maxima + jnp.log(totals)
    attn_probs = (exponent / totals).astype(jnp.bfloat16)
    attended = jnp.einsum(
        "grqk,kgd->qgrd", attn_probs, value_rows, preferred_element_type=jnp.float32
    )
    attended = attended.reshape(tok_rows, head_count * HD).astype(jnp.bfloat16)
    residual = inputs + jnp.dot(attended, w_out, preferred_element_type=jnp.float32)
    scale_ffn = rms_scale(residual)
    normed_ffn = (residual * scale_ffn * gain_ffn).astype(jnp.bfloat16)
    sent_rows, cot_all = lax.optimization_barrier((normed_ffn, cot_all))
    normed_all = lax.all_gather(sent_rows, "expert")
    earlier = (places[:, None] < places[None, :]).astype(jnp.bfloat16)
    expert_ids = jnp.arange(EXPERTS, dtype=jnp.int32)
    chosen = jnp.any(picks_all[:, :, None, :] == expert_ids[None, None, :, None], axis=1)
    own_ids = owner * local_experts
    hits = lax.dynamic_slice_in_dim(chosen, own_ids, local_experts, axis=1)
    ranks = jnp.einsum(
        "set,tu->seu", hits.astype(jnp.bfloat16), earlier, preferred_element_type=jnp.float32
    ).astype(jnp.int32)
    ranks = jnp.where(hits, ranks, -1)
    takes = ranks[:, :, None, :] == jnp.arange(CAP, dtype=jnp.int32)[None, None, :, None]
    one_hot = takes.astype(jnp.bfloat16)
    grad_taken = jnp.einsum(
        "sect,std->secd", one_hot, cot_all, preferred_element_type=jnp.float32
    ).astype(jnp.bfloat16)
    logits = jnp.einsum("std,de->set", normed_all, w_router, preferred_element_type=jnp.float32)
    logits = jnp.where(chosen, logits, -1e30)
    gate_exp = jnp.exp(logits - jnp.max(logits, axis=1, keepdims=True))
    gate_exp = jnp.where(chosen, gate_exp, 0.0)
    gates = gate_exp / jnp.sum(gate_exp, axis=1, keepdims=True)
    own_gates = lax.dynamic_slice_in_dim(gates, own_ids, local_experts, axis=1)
    gated = jnp.where(takes, own_gates[:, :, None, :], 0.0)
    slot_gate = jnp.sum(gated, axis=3)
    arrived = jnp.einsum(
        "sect,std->secd", one_hot, normed_all, preferred_element_type=jnp.float32
    ).astype(jnp.bfloat16)
    gate_pre, up_pre, hidden = expert_forward(arrived, w_gate, w_up)
    result = jnp.einsum(
        "secf,efd->secd", hidden, w_down, preferred_element_type=jnp.float32
    ).astype(jnp.bfloat16)
    expert_part = jnp.einsum(
        "sect,secd->std", gated.astype(jnp.bfloat16), result, preferred_element_type=jnp.float32
    ).astype(jnp.bfloat16)
    expert_part, grad_taken = lax.optimization_barrier((expert_part, grad_taken))
    expert_sum = lax.psum_scatter(
        expert_part.reshape(owner_count * tok_rows, width),
        "expert",
        scatter_dimension=0,
        tiled=True,
    )
    out_tokens = (residual + expert_sum.astype(jnp.float32)).astype(jnp.bfloat16)
    grad_flow = cotangent.astype(jnp.float32)
    slot_dots = jnp.sum(grad_taken.astype(jnp.float32) * result.astype(jnp.float32), axis=3)
    grad_gates = jnp.sum(jnp.where(takes, slot_dots[:, :, :, None], 0.0), axis=2)
    grad_gates = lax.all_to_all(grad_gates, "expert", split_axis=0, concat_axis=0, tiled=True)
    grad_gates = grad_gates.reshape(EXPERTS, tok_rows)
    back_grad = (grad_taken.astype(jnp.float32) * slot_gate[:, :, :, None]).astype(jnp.bfloat16)
    grad_hidden = jnp.einsum(
        "secd,efd->secf", back_grad, w_down, preferred_element_type=jnp.float32
    )
    sigmoid_gate = jax.nn.sigmoid(gate_pre)
    grad_gate_pre = (
        grad_hidden * up_pre * sigmoid_gate * (1.0 + gate_pre * (1.0 - sigmoid_gate))
    ).astype(jnp.bfloat16)
    grad_up_pre = (grad_hidden * gate_pre * sigmoid_gate).astype(jnp.bfloat16)
    grad_slots = jnp.einsum(
        "secf,edf->secd", grad_gate_pre, w_gate, preferred_element_type=jnp.float32
    )
    grad_slots = (
        grad_slots
        + jnp.einsum("secf,edf->secd", grad_up_pre, w_up, preferred_element_type=jnp.float32)
    ).astype(jnp.bfloat16)
    grad_part = jnp.einsum(
        "sect,secd->std", one_hot, grad_slots, preferred_element_type=jnp.float32
    ).astype(jnp.bfloat16)
    grad_rows = lax.psum_scatter(
        grad_part.reshape(owner_count * tok_rows, width),
        "expert",
        scatter_dimension=0,
        tiled=True,
    )
    grad_down = jnp.einsum("secf,secd->efd", hidden, back_grad, preferred_element_type=jnp.float32)
    grad_gate = jnp.einsum(
        "secd,secf->edf", arrived, grad_gate_pre, preferred_element_type=jnp.float32
    )
    grad_up = jnp.einsum("secd,secf->edf", arrived, grad_up_pre, preferred_element_type=jnp.float32)
    grad_gate, grad_up, grad_down = (
        item.astype(jnp.bfloat16) for item in (grad_gate, grad_up, grad_down)
    )
    grad_rows = lax.optimization_barrier((grad_rows, grad_gate, grad_up, grad_down))[0]
    grad_gate, grad_up, grad_down = (
        lax.psum_scatter(
            grad_gate, "dp", scatter_dimension=1, tiled=True
        ).astype(jnp.float32),
        lax.psum_scatter(
            grad_up, "dp", scatter_dimension=1, tiled=True
        ).astype(jnp.float32),
        lax.psum_scatter(
            grad_down, "dp", scatter_dimension=1, tiled=True
        ).astype(jnp.float32),
    )
    gate_vals = lax.dynamic_index_in_dim(gates, owner, axis=0, keepdims=False)
    grad_logits = (
        gate_vals * (grad_gates - jnp.sum(gate_vals * grad_gates, axis=0, keepdims=True))
    ).astype(jnp.bfloat16)
    grad_router = jnp.einsum(
        "et,td->de", grad_logits, normed_ffn, preferred_element_type=jnp.float32
    )
    grad_normed_ffn = jnp.einsum(
        "et,de->td", grad_logits, w_router, preferred_element_type=jnp.float32
    )
    grad_normed_ffn = grad_normed_ffn + grad_rows.astype(jnp.float32)
    grad_norm_part, grad_gain_ffn = rms_back(residual, scale_ffn, gain_ffn, grad_normed_ffn)
    grad_residual = grad_flow + grad_norm_part
    grad_branch = grad_residual.astype(jnp.bfloat16)
    grad_w_out = jnp.einsum("se,sd->ed", attended, grad_branch, preferred_element_type=jnp.float32)
    grad_attended = jnp.einsum("sd,ed->se", grad_branch, w_out, preferred_element_type=jnp.float32)
    grad_attended = grad_attended.astype(jnp.bfloat16).reshape(
        tok_rows, group_count, group_size, HD
    )
    again_probs = jnp.exp(masked_scores(queries, key_rows, allowed) - log_totals)
    grad_probs = jnp.einsum(
        "qgrd,kgd->grqk", grad_attended, value_rows, preferred_element_type=jnp.float32
    )
    grad_scores = (
        again_probs * (grad_probs - jnp.sum(again_probs * grad_probs, axis=-1, keepdims=True))
    ).astype(jnp.bfloat16)
    grad_q = (
        jnp.einsum("grqk,kgd->qgrd", grad_scores, key_rows, preferred_element_type=jnp.float32)
        * 0.125
    )
    grad_k = (
        jnp.einsum("grqk,qgrd->kgd", grad_scores, queries, preferred_element_type=jnp.float32)
        * 0.125
    )
    grad_v = jnp.einsum(
        "grqk,qgrd->kgd",
        again_probs.astype(jnp.bfloat16),
        grad_attended,
        preferred_element_type=jnp.float32,
    )
    grad_q = (
        rotate(grad_q.reshape(tok_rows, head_count, HD), cosine, -sine_part)
        .reshape(tok_rows, head_count * HD)
        .astype(jnp.bfloat16)
    )
    grad_k = (
        rotate(grad_k, cosine, -sine_part).reshape(tok_rows, group_count * HD).astype(jnp.bfloat16)
    )
    grad_v = grad_v.reshape(tok_rows, group_count * HD).astype(jnp.bfloat16)
    grad_query = jnp.einsum("sd,se->de", normed_attn, grad_q, preferred_element_type=jnp.float32)
    grad_key = jnp.einsum("sd,se->de", normed_attn, grad_k, preferred_element_type=jnp.float32)
    grad_value = jnp.einsum("sd,se->de", normed_attn, grad_v, preferred_element_type=jnp.float32)
    grad_normed_attn = jnp.einsum("se,de->sd", grad_q, w_query, preferred_element_type=jnp.float32)
    grad_normed_attn = grad_normed_attn + jnp.einsum(
        "se,de->sd", grad_k, w_key, preferred_element_type=jnp.float32
    )
    grad_normed_attn = grad_normed_attn + jnp.einsum(
        "se,de->sd", grad_v, w_value, preferred_element_type=jnp.float32
    )
    grad_input_part, grad_gain_attn = rms_back(inputs, scale_attn, gain_attn, grad_normed_attn)
    grad_tokens = (grad_residual + grad_input_part).astype(jnp.bfloat16)
    small = jnp.concatenate(
        [
            grad_router,
            grad_gain_attn[:, None],
            grad_gain_ffn[:, None],
            jnp.zeros((width, 128 - EXPERTS - 2), jnp.float32),
        ],
        axis=1,
    )
    sums = [
        item.astype(jnp.bfloat16)
        for item in (grad_query, grad_key, grad_value, grad_w_out, small)
    ]
    sums = lax.psum(tuple(lax.optimization_barrier(sums)), ("dp", "expert"))
    grad_query, grad_key, grad_value, grad_w_out, small = (
        item.astype(jnp.float32) for item in sums
    )
    grad_router = small[:, :EXPERTS]
    grad_gain_attn, grad_gain_ffn = small[:, EXPERTS], small[:, EXPERTS + 1]
    return (
        out_tokens,
        grad_tokens,
        grad_gain_attn,
        grad_query,
        grad_key,
        grad_value,
        grad_w_out,
        grad_gain_ffn,
        grad_router,
        grad_gate,
        grad_up,
        grad_down,
    )


def solution(mesh):
    placed = (
        P(("dp", "expert"), None),
        P(("dp", "expert"), None),
        P(("dp", "expert"), None),
        P(),
        P(),
        P(),
        P(),
        P(),
        P(),
        P(),
        P("expert", None, None),
        P("expert", None, None),
        P("expert", None, None),
        P(("dp", "expert"), None),
    )
    return jax.shard_map(
        shards,
        mesh=mesh,
        in_specs=placed,
        out_specs=(
            P(("dp", "expert"), None),
            P(("dp", "expert"), None),
            P(),
            P(),
            P(),
            P(),
            P(),
            P(),
            P(),
            P("expert", "dp", None),
            P("expert", "dp", None),
            P("expert", "dp", None),
        ),
        check_vma=False,
    )
```
